32 devices in a mesh: slab: 8 (over z, x), row: 4 (over y, core).
Axes of the slice: x: 2, y: 2, z: 4, core: 2. Of those that a mesh axis runs over, the one named last changes fastest.
Arguments:
- panel: bfloat16 [8, 16, 128, 256], P('slab', 'row'), may hold values from -6 to 6
- blocks: bfloat16 [8, 16, 6, 128, 128], P('slab', 'row'), may hold values from -0.109375 to 0.109375
- offsets: int32 [8, 16, 6], P('slab', 'row'), may hold values from 0 to 8
- stiff_diag: float32 [8, 16, 128], P('slab', 'row'), may hold values from 1 to 3
- base_mass: float32 [8, 16, 128], P('slab', 'row'), may hold values from 1 to 6
- mistune: float32 [16, 128], replicated, may hold values from 0.5 to 1.5
- pattern: int32 [8, 16], P('slab', 'row'), may hold values from 0 to 15
Outputs:
- ritz_basis: float32 [8, 16, 128, 256], P('slab', 'row')
- ritz_matrix: float32 [256, 256], replicated
- stiff_image: float32 [8, 16, 128, 256], P('slab', 'row')
The draws below stay inside these ranges and needn't reach their ends.
All inputs are finite; a program needn't handle non-finite values.
Results may differ from the reference program's by a relative error of at most 0.0013.
Values may be sent and summed in bfloat16 or wider, within the bound.
A program may use at most 64 MiB of HBM per device.

```python
import math
import jax
import jax.numpy as jnp
from jax import lax

BS = 128
NV = 256
NNZB = 6
DEG = 8
NPAT = 16
GSALL = 8
GRALL = 16
NALL = 16384


def draw_base_mass(key, part):
    key = jax.random.fold_in(key, 11)
    shape = (GSALL, GRALL, BS)
    position = jnp.arange(GSALL, dtype=jnp.float32)[:, None, None] / GSALL
    spread = jnp.exp(jax.random.uniform(key, shape, jnp.float32, 0.0, math.log(2.0)))
    return spread * jnp.exp(math.log(3.0) * position)


def with_ends(array, own_key, least, top_value):
    place = [jax.random.randint(jax.random.fold_in(own_key, axis), (), 0, length) for axis, length in enumerate(array.shape)]
    widest = array.shape.index(max(array.shape))
    beside = place[:widest] + [(place[widest] + 1) % array.shape[widest]] + place[widest + 1:]
    return array.at[tuple(place)].set(least).at[tuple(beside)].set(top_value)


def block_scale(stream_key, shape, pieces, low, largest):
    loudness = 1.0
    for dim, parts in pieces:
        steps = jax.random.uniform(jax.random.fold_in(jax.random.fold_in(stream_key, 6), dim), (parts,), jnp.float32, low / len(pieces), largest / len(pieces))
        loudness = loudness * jnp.repeat(jnp.exp(steps), shape[dim] // parts).reshape((-1,) + (1,) * (len(shape) - 1 - dim))
    return loudness


def noise(rng, extent, scale, most, split=(), held_as=jnp.bfloat16):
    factor_of = block_scale(rng, extent, split, -0.22, 0.18) if split else 1.0
    array = jax.random.normal(rng, extent, jnp.float32) * scale * factor_of
    return jnp.minimum(jnp.maximum(array, -most), most).astype(held_as)


def setup_inputs(seed: int = 0) -> dict:
    splits = jax.random.split(jax.random.key(seed), 8)
    panel = noise(splits[0], (GSALL, GRALL, BS, NV), 1.0, 6.0, ((0, 8), (1, 4)))
    blocks = noise(splits[1], (GSALL, GRALL, NNZB, BS, BS), (4 * NNZB * BS) ** -0.5, 0.109375, ((0, 8), (1, 4)))
    offsets = with_ends(jax.random.randint(splits[2], (GSALL, GRALL, NNZB), 0, 9), jax.random.fold_in(splits[2], 1), 0, 8).astype(jnp.int32)
    stiff_diag = jnp.clip(jnp.exp(math.log(3.0) - 1.0986123 * jax.random.uniform(splits[3], (GSALL, GRALL, BS), jnp.float32) ** block_scale(splits[3], (GSALL, GRALL, BS), ((0, 8), (1, 4)), -0.2, 0.2)), 1.0, 3.0)
    base_mass = draw_base_mass(jax.random.fold_in(splits[7], 71), 0)
    mistune = jnp.clip(1.0 + 0.1 * jax.random.normal(splits[5], (NPAT, BS), jnp.float32), 0.5, 1.5)
    pattern = with_ends(jax.random.randint(splits[6], (GSALL, GRALL), 0, NPAT), jax.random.fold_in(splits[6], 1), 0, NPAT - 1).astype(jnp.int32)
    return dict(panel=panel, blocks=blocks, offsets=offsets, stiff_diag=stiff_diag, base_mass=base_mass, mistune=mistune, pattern=pattern)


highest = lax.Precision.HIGHEST
lower_edge = 2.5
upper_edge = 12.0
anchor_point = 0.0

def filter_scales(degree):
    half_width = (upper_edge - lower_edge) / 2.0
    centre_point = (upper_edge + lower_edge) / 2.0
    first_scale = half_width / (anchor_point - centre_point)
    doubled = 2.0 / first_scale
    scales = [(first_scale / half_width, 0.0)]
    previous = first_scale
    for section in range(1, degree):
        current = 1.0 / (doubled - previous)
        scales.append((2.0 * current / half_width, previous * current))
        previous = current
    return (centre_point, scales)

def stiff_apply(field, blocks, offsets, stiff_diag):
    padded = jnp.pad(field, ((0, 0), (1, 1), (0, 0), (0, 0)))
    cross_ids = jnp.arange(GRALL, dtype=jnp.int32)[:, None]

    def one_slab(index):
        beside_all = (index + jnp.arange(3, dtype=jnp.int32) - 1) % GSALL
        nearby = jnp.take(padded, beside_all.astype(jnp.int32), axis=0)
        slot_ids = lax.dynamic_index_in_dim(offsets, index, 0, keepdims=False)
        picked = nearby[slot_ids // 3, cross_ids + slot_ids % 3]
        coupling = lax.dynamic_index_in_dim(blocks, index, 0, keepdims=False).astype(jnp.float32)
        return jnp.einsum('jsab,jsbv->jav', coupling, picked, precision=highest)
    coupled = lax.map(one_slab, jnp.arange(GSALL, dtype=jnp.int32))
    return stiff_diag[..., None] * field + coupled

def reference(panel, blocks, offsets, stiff_diag, base_mass, mistune, pattern):
    mass = base_mass * mistune[pattern]
    inv_mass = 1.0 / mass
    centre_point, scales = filter_scales(DEG)
    current = panel.astype(jnp.float32)
    previous = jnp.zeros_like(current)
    for section in range(DEG):
        rounded = current.astype(jnp.bfloat16)
        rounded = lax.optimization_barrier(rounded)
        image = inv_mass[..., None] * stiff_apply(rounded.astype(jnp.float32), blocks, offsets, stiff_diag)
        gain_factor, carry_factor = scales[section]
        following = gain_factor * (image - centre_point * current) - carry_factor * previous
        previous = current
        current = following
    filtered = current
    flat = filtered.reshape(-1, NV)
    weighted = (mass[..., None] * filtered).reshape(-1, NV)
    mass_gram = jnp.einsum('rv,rw->vw', weighted, flat, precision=highest) / NALL
    k_field = stiff_apply(filtered, blocks, offsets, stiff_diag).reshape(-1, NV)
    stiff_gram = jnp.einsum('rv,rw->vw', flat, k_field, precision=highest) / NALL
    lower_tri = jnp.linalg.cholesky(mass_gram)
    identity = jnp.eye(NV, dtype=jnp.float32)
    back = jax.scipy.linalg.solve_triangular(lower_tri, identity, lower=True).T
    ritz_basis = jnp.dot(flat, back, precision=highest).reshape(filtered.shape)
    ritz_matrix = jnp.dot(back.T, jnp.dot(stiff_gram, back, precision=highest), precision=highest)
    stiff_image = stiff_apply(ritz_basis, blocks, offsets, stiff_diag)
    return (ritz_basis, ritz_matrix, stiff_image)
```

```python
import functools

import jax
import jax.numpy as jnp
from jax import lax
from jax.experimental import pallas as pl
from jax.experimental.pallas import tpu as pltpu
from jax.sharding import PartitionSpec as P

DEG = 8
MESH = pl.DeviceIdType.MESH

highest = lax.Precision.HIGHEST
lower_edge = 2.5
upper_edge = 12.0
anchor_point = 0.0


def filter_scales(degree):
    half_width = (upper_edge - lower_edge) / 2.0
    centre_point = (upper_edge + lower_edge) / 2.0
    first_scale = half_width / (anchor_point - centre_point)
    doubled = 2.0 / first_scale
    scales = [(first_scale / half_width, 0.0)]
    previous = first_scale
    for section in range(1, degree):
        current = 1.0 / (doubled - previous)
        scales.append((2.0 * current / half_width, previous * current))
        previous = current
    return (centre_point, scales)


def neighbour_index(offsets, cross_blocks):
    cross_pos = jnp.arange(cross_blocks, dtype=jnp.int32)[None, :, None]
    return ((offsets // 3) * (cross_blocks + 2) + cross_pos + offsets % 3).reshape(-1)


def split3_dot(a, b, dims):
    a_hi = a.astype(jnp.bfloat16)
    b_hi = b.astype(jnp.bfloat16)
    a_lo = (a - a_hi.astype(jnp.float32)).astype(jnp.bfloat16)
    b_lo = (b - b_hi.astype(jnp.float32)).astype(jnp.bfloat16)
    dot = functools.partial(
        lax.dot_general, dimension_numbers=(dims, ((), ())), preferred_element_type=jnp.float32
    )
    return dot(a_hi, b_hi) + (dot(a_hi, b_lo) + dot(a_lo, b_hi))


def filter_kernel(
    slabs, rows, cols, slots, halves, lanes,
    index_ref, panel_ref, blocks_ref, inv_ref, diag_ref, mass_ref,
    y_ref, ky_ref, gram_ref,
    ext00, ext01, ext10, ext11, prev_ref, slab_send, slab_recv, row_send, row_recv,
):
    wide = cols + 2
    first = wide + 1
    ext = ((ext00, ext01), (ext10, ext11))
    s = lax.axis_index("slab")
    r = lax.axis_index("row")
    up = lax.rem(s + 1, slabs)
    down = lax.rem(s + slabs - 1, slabs)
    has_left = r > 0
    has_right = r < rows - 1
    centre, scales = filter_scales(DEG)

    barrier = pltpu.get_barrier_semaphore()
    pl.semaphore_signal(barrier, inc=1, device_id=(up, r), device_id_type=MESH)
    pl.semaphore_signal(barrier, inc=1, device_id=(down, r), device_id_type=MESH)

    @pl.when(has_left)
    def _():
        pl.semaphore_signal(barrier, inc=1, device_id=(s, r - 1), device_id_type=MESH)

    @pl.when(has_right)
    def _():
        pl.semaphore_signal(barrier, inc=1, device_id=(s, r + 1), device_id_type=MESH)

    def slab_copies(t):
        p, h = (t // halves) % 2, t % halves
        buf = ext[p][h]
        own = buf.at[pl.ds(first, cols)]
        return [
            pltpu.make_async_remote_copy(
                src_ref=own, dst_ref=buf.at[pl.ds(1 + 2 * wide * lower, cols)],
                send_sem=slab_send.at[p, h, lower], recv_sem=slab_recv.at[p, h, lower],
                device_id=(target, r), device_id_type=MESH,
            )
            for lower, target in ((0, up), (1, down))
        ]

    def row_copies(t, side):
        p, h = (t // halves) % 2, t % halves
        buf = ext[p][h]
        source, place, target = ((cols, 0, r + 1), (1, cols + 1, r - 1))[side]
        return [
            pltpu.make_async_remote_copy(
                src_ref=buf.at[pl.ds(source + wide * k, 1)], dst_ref=buf.at[pl.ds(place + wide * k, 1)],
                send_sem=row_send.at[p, h, side, k], recv_sem=row_recv.at[p, h, side, k],
                device_id=(s, target), device_id_type=MESH,
            )
            for k in range(3)
        ]

    def start_slab(t):
        for copy in slab_copies(t):
            copy.start()

    def wait_slab(t):
        for copy in slab_copies(t):
            copy.wait()

    def start_row(t):
        for side, there in ((0, has_right), (1, has_left)):
            @pl.when(there)
            def _():
                for copy in row_copies(t, side):
                    copy.start()

    def wait_row(t):
        for side, there in ((0, has_right), (1, has_left)):
            @pl.when(there)
            def _():
                for copy in row_copies(t, side):
                    copy.wait_send()
                for copy in row_copies(t, 1 - side):
                    copy.wait_recv()

    def compute(t):
        k, h = t // halves, t % halves
        buf = ext[k % 2][h]
        nxt = ext[(k + 1) % 2][h]
        span = pl.ds(h * lanes, lanes)

        def one(c, carry):
            acc = diag_ref[c] * buf[first + c].astype(jnp.float32) if k < DEG else diag_ref[c] * y_ref[c, :, span]
            for slot in range(slots):
                acc += jnp.dot(
                    blocks_ref[c, slot], buf[index_ref[c * slots + slot]], preferred_element_type=jnp.float32
                )
            if k < DEG:
                gain, back = scales[k]
                cur = y_ref[c, :, span]
                new = gain * (inv_ref[c] * acc - centre * cur)
                if k > 0:
                    new -= back * prev_ref[c, :, span]
                prev_ref[c, :, span] = cur
                y_ref[c, :, span] = new
                nxt[first + c] = new.astype(jnp.bfloat16)
            else:
                ky_ref[c, :, span] = acc
            return carry

        lax.fori_loop(0, cols, one, 0)

    for p in range(2):
        for h in range(halves):
            @pl.when(jnp.logical_not(has_left))
            def _():
                for k in range(3):
                    ext[p][h][wide * k] = jnp.zeros(ext00.shape[1:], jnp.bfloat16)

            @pl.when(jnp.logical_not(has_right))
            def _():
                for k in range(3):
                    ext[p][h][wide * k + cols + 1] = jnp.zeros(ext00.shape[1:], jnp.bfloat16)

    for h in range(halves):
        for c in range(cols):
            ext[0][h][first + c] = panel_ref[c, :, h * lanes:(h + 1) * lanes]

    pl.semaphore_wait(barrier, 2 + (r + rows - 1) // rows + (2 * rows - 2 - r) // rows)

    for h in range(halves):
        start_slab(h)
    y_ref[...] = panel_ref[...].astype(jnp.float32)
    total = halves * (DEG + 1)
    vectors = y_ref.shape[-1]
    depth = cols * y_ref.shape[1]
    for t in range(total + 1):
        if t >= 1:
            wait_row(t - 1)
            compute(t - 1)
            if halves <= t - 1 + halves < total:
                start_slab(t - 1 + halves)
            if t - 1 == halves * DEG - 1:
                flat = y_ref[...].reshape(depth, vectors)
                weight = mass_ref[...].reshape(depth, lanes)
                weighted = jnp.concatenate([weight] * halves, axis=1) * flat
                gram_ref[:vectors] = split3_dot(weighted, flat, ((0,), (0,)))
        if t < total:
            wait_slab(t)
            start_row(t)
    gram_ref[vectors:] = split3_dot(
        y_ref[...].reshape(depth, vectors), ky_ref[...].reshape(depth, vectors), ((0,), (0,))
    )


def sum_kernel(slabs, rows, g_ref, out_ref, first, parts, total, pair_send, pair_recv, a_send, a_recv, b_send, b_recv):
    half = g_ref.shape[0] // 2
    group = slabs * (rows // 2)
    chunk = half // group
    s = lax.axis_index("slab")
    r = lax.axis_index("row")
    core = lax.rem(r, 2)
    me = s * (rows // 2) + r // 2
    partner = (s, r + 1 - 2 * core)

    def member(d):
        q = lax.rem(me + d, group)
        return (q // (rows // 2), lax.rem(q, rows // 2) * 2 + core)

    barrier = pltpu.get_barrier_semaphore()
    pl.semaphore_signal(barrier, inc=1, device_id=partner, device_id_type=MESH)
    for d in range(1, group):
        pl.semaphore_signal(barrier, inc=1, device_id=member(d), device_id_type=MESH)
    pl.semaphore_wait(barrier, group)

    mine = pl.ds(pl.multiple_of(core * half, half), half)
    theirs = pl.ds(pl.multiple_of((1 - core) * half, half), half)
    swap = pltpu.make_async_remote_copy(
        src_ref=g_ref.at[theirs], dst_ref=first, send_sem=pair_send.at[0], recv_sem=pair_recv.at[0],
        device_id=partner, device_id_type=MESH,
    )
    swap.start()
    swap.wait()
    first[...] += g_ref[mine]
    copies = []
    for d in range(1, group):
        q = lax.rem(me + d, group)
        copy = pltpu.make_async_remote_copy(
            src_ref=first.at[pl.ds(pl.multiple_of(q * chunk, chunk), chunk)], dst_ref=parts.at[d],
            send_sem=a_send.at[d], recv_sem=a_recv.at[d], device_id=member(d), device_id_type=MESH,
        )
        copy.start()
        copies.append(copy)
    acc = first[pl.ds(pl.multiple_of(me * chunk, chunk), chunk)]
    for d, copy in enumerate(copies, 1):
        copy.wait()
        acc += parts[d]
    spot = pl.ds(pl.multiple_of(core * half + me * chunk, chunk), chunk)
    total[spot] = acc
    copies = []
    for d in range(1, group):
        copy = pltpu.make_async_remote_copy(
            src_ref=total.at[spot], dst_ref=total.at[spot],
            send_sem=b_send.at[d], recv_sem=b_recv.at[d], device_id=member(d), device_id_type=MESH,
        )
        copy.start()
        copies.append(copy)
    for copy in copies:
        copy.wait()
    swap = pltpu.make_async_remote_copy(
        src_ref=total.at[mine], dst_ref=total.at[mine], send_sem=pair_send.at[1], recv_sem=pair_recv.at[1],
        device_id=partner, device_id_type=MESH,
    )
    swap.start()
    swap.wait()
    out_ref[...] = total[...]


def sum_everywhere(grams, slabs, rows):
    height, width = grams.shape
    group = slabs * rows // 2
    if rows % 2 or height % (2 * group) or (height // (2 * group)) % 8:
        return lax.psum(grams, ("slab", "row"))
    half = height // 2
    vmem = pl.BlockSpec(memory_space=pltpu.VMEM)
    return pl.pallas_call(
        functools.partial(sum_kernel, slabs, rows),
        out_shape=jax.ShapeDtypeStruct(grams.shape, jnp.float32),
        in_specs=[vmem],
        out_specs=vmem,
        scratch_shapes=[
            pltpu.VMEM((half, width), jnp.float32),
            pltpu.VMEM((group, half // group, width), jnp.float32),
            pltpu.VMEM((height, width), jnp.float32),
            pltpu.SemaphoreType.DMA((2,)),
            pltpu.SemaphoreType.DMA((2,)),
            pltpu.SemaphoreType.DMA((group,)),
            pltpu.SemaphoreType.DMA((group,)),
            pltpu.SemaphoreType.DMA((group,)),
            pltpu.SemaphoreType.DMA((group,)),
        ],
        compiler_params=pltpu.CompilerParams(
            collective_id=1, has_side_effects=True, vmem_limit_bytes=16 * 1024 * 1024
        ),
        name="sum_everywhere",
    )(grams)


def shards(slabs, rows, panel, blocks, offsets, stiff_diag, base_mass, mistune, pattern):
    _, cols, block_rows, vectors = panel.shape
    slots = blocks.shape[2]
    total_rows = cols * block_rows * slabs * rows
    levels = mistune.shape[0]
    one_hot = (pattern[:, :, None] == jnp.arange(levels, dtype=jnp.int32)).astype(jnp.float32)
    blade_factor = jnp.einsum("ijp,pb->ijb", one_hot, mistune, precision=highest)
    mass = (base_mass * blade_factor)[0]
    halves = 2
    lanes = vectors // halves
    spread = lambda a: jnp.broadcast_to(a[..., None], (cols, block_rows, lanes))
    vmem = pl.BlockSpec(memory_space=pltpu.VMEM)
    field = jax.ShapeDtypeStruct((cols, block_rows, vectors), jnp.float32)
    cells = 3 * (cols + 2)
    y, ky, grams = pl.pallas_call(
        functools.partial(filter_kernel, slabs, rows, cols, slots, halves, lanes),
        out_shape=(field, field, jax.ShapeDtypeStruct((2 * vectors, vectors), jnp.float32)),
        in_specs=[pl.BlockSpec(memory_space=pltpu.SMEM)] + [vmem] * 5,
        out_specs=(vmem, vmem, vmem),
        scratch_shapes=[pltpu.VMEM((cells, block_rows, lanes), jnp.bfloat16)] * 4
        + [
            pltpu.VMEM((cols, block_rows, vectors), jnp.float32),
            pltpu.SemaphoreType.DMA((2, halves, 2)),
            pltpu.SemaphoreType.DMA((2, halves, 2)),
            pltpu.SemaphoreType.DMA((2, halves, 2, 3)),
            pltpu.SemaphoreType.DMA((2, halves, 2, 3)),
        ],
        compiler_params=pltpu.CompilerParams(
            collective_id=0, has_side_effects=True, vmem_limit_bytes=32 * 1024 * 1024
        ),
        name="filter_and_grams",
    )(neighbour_index(offsets, cols), panel[0], blocks[0], spread(1.0 / mass), spread(stiff_diag[0]), spread(mass))
    grams = sum_everywhere(grams, slabs, rows) / total_rows
    mass_gram, stiff_gram = grams[:vectors], grams[vectors:]
    lower_tri = jnp.linalg.cholesky(mass_gram)
    identity = jnp.eye(vectors, dtype=jnp.float32)
    back = jax.scipy.linalg.solve_triangular(lower_tri, identity, lower=True).T
    flat = y.reshape(-1, vectors)
    ritz_basis = jnp.dot(flat, back, precision=highest).reshape((1,) + y.shape)
    stiff_image = jnp.dot(ky.reshape(-1, vectors), back, precision=highest).reshape((1,) + y.shape)
    ritz_matrix = jnp.dot(back.T, jnp.dot(stiff_gram, back, precision=highest), precision=highest)
    return (ritz_basis, ritz_matrix, stiff_image)


def solution(mesh):
    return jax.shard_map(
        functools.partial(shards, mesh.shape["slab"], mesh.shape["row"]),
        mesh=mesh,
        in_specs=(
            P("slab", "row", None, None),
            P("slab", "row", None, None, None),
            P("slab", "row", None),
            P("slab", "row", None),
            P("slab", "row", None),
            P(),
            P("slab", "row"),
        ),
        out_specs=(P("slab", "row", None, None), P(), P("slab", "row", None, None)),
        check_vma=False,
    )
```

```python
import functools

import jax
import jax.numpy as jnp
from jax import lax
from jax.experimental import pallas as pl
from jax.experimental.pallas import tpu as pltpu
from jax.sharding import PartitionSpec as P

DEG = 8
MESH = pl.DeviceIdType.MESH

highest = lax.Precision.HIGHEST
lower_edge = 2.5
upper_edge = 12.0
anchor_point = 0.0


def filter_scales(degree):
    half_width = (upper_edge - lower_edge) / 2.0
    centre_point = (upper_edge + lower_edge) / 2.0
    first_scale = half_width / (anchor_point - centre_point)
    doubled = 2.0 / first_scale
    scales = [(first_scale / half_width, 0.0)]
    previous = first_scale
    for section in range(1, degree):
        current = 1.0 / (doubled - previous)
        scales.append((2.0 * current / half_width, previous * current))
        previous = current
    return (centre_point, scales)


def neighbour_index(offsets, cross_blocks):
    cross_pos = jnp.arange(cross_blocks, dtype=jnp.int32)[None, :, None]
    return ((offsets // 3) * (cross_blocks + 2) + cross_pos + offsets % 3).reshape(-1)


def split3_dot(a, b, dims):
    a_hi = a.astype(jnp.bfloat16)
    b_hi = b.astype(jnp.bfloat16)
    a_lo = (a - a_hi.astype(jnp.float32)).astype(jnp.bfloat16)
    b_lo = (b - b_hi.astype(jnp.float32)).astype(jnp.bfloat16)
    dot = functools.partial(
        lax.dot_general, dimension_numbers=(dims, ((), ())), preferred_element_type=jnp.float32
    )
    return dot(a_hi, b_hi) + (dot(a_hi, b_lo) + dot(a_lo, b_hi))


def filter_kernel(
    slabs, rows, cols, slots, halves, lanes,
    index_ref, panel_ref, blocks_ref, inv_ref, diag_ref, mass_ref,
    y_ref, ky_ref, gram_ref,
    ext00, ext01, ext10, ext11, prev_ref, slab_send, slab_recv, row_send, row_recv,
):
    wide = cols + 2
    first = wide + 1
    ext = ((ext00, ext01), (ext10, ext11))
    s = lax.axis_index("slab")
    r = lax.axis_index("row")
    up = lax.rem(s + 1, slabs)
    down = lax.rem(s + slabs - 1, slabs)
    has_left = r > 0
    has_right = r < rows - 1
    centre, scales = filter_scales(DEG)

    barrier = pltpu.get_barrier_semaphore()
    pl.semaphore_signal(barrier, inc=1, device_id=(up, r), device_id_type=MESH)
    pl.semaphore_signal(barrier, inc=1, device_id=(down, r), device_id_type=MESH)

    @pl.when(has_left)
    def _():
        pl.semaphore_signal(barrier, inc=1, device_id=(s, r - 1), device_id_type=MESH)

    @pl.when(has_right)
    def _():
        pl.semaphore_signal(barrier, inc=1, device_id=(s, r + 1), device_id_type=MESH)

    def slab_copies(t):
        p, h = (t // halves) % 2, t % halves
        buf = ext[p][h]
        own = buf.at[pl.ds(first, cols)]
        return [
            pltpu.make_async_remote_copy(
                src_ref=own, dst_ref=buf.at[pl.ds(1 + 2 * wide * lower, cols)],
                send_sem=slab_send.at[p, h, lower], recv_sem=slab_recv.at[p, h, lower],
                device_id=(target, r), device_id_type=MESH,
            )
            for lower, target in ((0, up), (1, down))
        ]

    def row_copies(t, side):
        p, h = (t // halves) % 2, t % halves
        buf = ext[p][h]
        source, place, target = ((cols, 0, r + 1), (1, cols + 1, r - 1))[side]
        return [
            pltpu.make_async_remote_copy(
                src_ref=buf.at[pl.ds(source + wide * k, 1)], dst_ref=buf.at[pl.ds(place + wide * k, 1)],
                send_sem=row_send.at[p, h, side, k], recv_sem=row_recv.at[p, h, side, k],
                device_id=(s, target), device_id_type=MESH,
            )
            for k in range(3)
        ]

    def start_slab(t):
        for copy in slab_copies(t):
            copy.start()

    def wait_slab(t):
        for copy in slab_copies(t):
            copy.wait()

    def start_row(t):
        for side, there in ((0, has_right), (1, has_left)):
            @pl.when(there)
            def _():
                for copy in row_copies(t, side):
                    copy.start()

    def wait_row(t):
        for side, there in ((0, has_right), (1, has_left)):
            @pl.when(there)
            def _():
                for copy in row_copies(t, side):
                    copy.wait_send()
                for copy in row_copies(t, 1 - side):
                    copy.wait_recv()

    def compute(t):
        k, h = t // halves, t % halves
        buf = ext[k % 2][h]
        nxt = ext[(k + 1) % 2][h]
        span = pl.ds(h * lanes, lanes)

        def one(c, carry):
            acc = diag_ref[c] * buf[first + c].astype(jnp.float32) if k < DEG else diag_ref[c] * y_ref[c, :, span]
            for slot in range(slots):
                acc += jnp.dot(
                    blocks_ref[c, slot], buf[index_ref[c * slots + slot]], preferred_element_type=jnp.float32
                )
            if k < DEG:
                gain, back = scales[k]
                cur = y_ref[c, :, span]
                new = gain * (inv_ref[c] * acc - centre * cur)
                if k > 0:
                    new -= back * prev_ref[c, :, span]
                prev_ref[c, :, span] = cur
                y_ref[c, :, span] = new
                nxt[first + c] = new.astype(jnp.bfloat16)
            else:
                ky_ref[c, :, span] = acc
            return carry

        lax.fori_loop(0, cols, one, 0)

    for p in range(2):
        for h in range(halves):
            @pl.when(jnp.logical_not(has_left))
            def _():
                for k in range(3):
                    ext[p][h][wide * k] = jnp.zeros(ext00.shape[1:], jnp.bfloat16)

            @pl.when(jnp.logical_not(has_right))
            def _():
                for k in range(3):
                    ext[p][h][wide * k + cols + 1] = jnp.zeros(ext00.shape[1:], jnp.bfloat16)

    for h in range(halves):
        for c in range(cols):
            ext[0][h][first + c] = panel_ref[c, :, h * lanes:(h + 1) * lanes]

    pl.semaphore_wait(barrier, 2 + (r + rows - 1) // rows + (2 * rows - 2 - r) // rows)

    for h in range(halves):
        start_slab(h)
    y_ref[...] = panel_ref[...].astype(jnp.float32)
    total = halves * (DEG + 1)
    vectors = y_ref.shape[-1]
    depth = cols * y_ref.shape[1]
    for t in range(total + 1):
        if t >= 1:
            wait_row(t - 1)
            compute(t - 1)
            if halves <= t - 1 + halves < total:
                start_slab(t - 1 + halves)
            if t - 1 == halves * DEG - 1:
                flat = y_ref[...].reshape(depth, vectors)
                weight = mass_ref[...].reshape(depth, lanes)
                weighted = jnp.concatenate([weight] * halves, axis=1) * flat
                gram_ref[:vectors] = split3_dot(weighted, flat, ((0,), (0,)))
        if t < total:
            wait_slab(t)
            start_row(t)
    gram_ref[vectors:] = split3_dot(
        y_ref[...].reshape(depth, vectors), ky_ref[...].reshape(depth, vectors), ((0,), (0,))
    )


def sum_kernel(slabs, rows, g_ref, out_ref, first, parts, total, pair_send, pair_recv, a_send, a_recv, b_send, b_recv):
    half = g_ref.shape[0] // 2
    group = slabs * (rows // 2)
    chunk = half // group
    s = lax.axis_index("slab")
    r = lax.axis_index("row")
    core = lax.rem(r, 2)
    me = s * (rows // 2) + r // 2
    partner = (s, r + 1 - 2 * core)

    def member(d):
        q = lax.rem(me + d, group)
        return (q // (rows // 2), lax.rem(q, rows // 2) * 2 + core)

    barrier = pltpu.get_barrier_semaphore()
    pl.semaphore_signal(barrier, inc=1, device_id=partner, device_id_type=MESH)
    for d in range(1, group):
        pl.semaphore_signal(barrier, inc=1, device_id=member(d), device_id_type=MESH)
    pl.semaphore_wait(barrier, group)

    mine = pl.ds(pl.multiple_of(core * half, half), half)
    theirs = pl.ds(pl.multiple_of((1 - core) * half, half), half)
    swap = pltpu.make_async_remote_copy(
        src_ref=g_ref.at[theirs], dst_ref=first, send_sem=pair_send.at[0], recv_sem=pair_recv.at[0],
        device_id=partner, device_id_type=MESH,
    )
    swap.start()
    swap.wait()
    first[...] += g_ref[mine]
    copies = []
    for d in range(1, group):
        q = lax.rem(me + d, group)
        copy = pltpu.make_async_remote_copy(
            src_ref=first.at[pl.ds(pl.multiple_of(q * chunk, chunk), chunk)], dst_ref=parts.at[d],
            send_sem=a_send.at[d], recv_sem=a_recv.at[d], device_id=member(d), device_id_type=MESH,
        )
        copy.start()
        copies.append(copy)
    acc = first[pl.ds(pl.multiple_of(me * chunk, chunk), chunk)]
    for d, copy in enumerate(copies, 1):
        copy.wait()
        acc += parts[d]
    spot = pl.ds(pl.multiple_of(core * half + me * chunk, chunk), chunk)
    total[spot] = acc
    copies = []
    for d in range(1, group):
        copy = pltpu.make_async_remote_copy(
            src_ref=total.at[spot], dst_ref=total.at[spot],
            send_sem=b_send.at[d], recv_sem=b_recv.at[d], device_id=member(d), device_id_type=MESH,
        )
        copy.start()
        copies.append(copy)
    for copy in copies:
        copy.wait()
    swap = pltpu.make_async_remote_copy(
        src_ref=total.at[mine], dst_ref=total.at[mine], send_sem=pair_send.at[1], recv_sem=pair_recv.at[1],
        device_id=partner, device_id_type=MESH,
    )
    swap.start()
    swap.wait()
    out_ref[...] = total[...]


def sum_everywhere(grams, slabs, rows):
    height, width = grams.shape
    group = slabs * rows // 2
    if rows % 2 or height % (2 * group) or (height // (2 * group)) % 8:
        return lax.psum(grams, ("slab", "row"))
    half = height // 2
    vmem = pl.BlockSpec(memory_space=pltpu.VMEM)
    return pl.pallas_call(
        functools.partial(sum_kernel, slabs, rows),
        out_shape=jax.ShapeDtypeStruct(grams.shape, jnp.float32),
        in_specs=[vmem],
        out_specs=vmem,
        scratch_shapes=[
            pltpu.VMEM((half, width), jnp.float32),
            pltpu.VMEM((group, half // group, width), jnp.float32),
            pltpu.VMEM((height, width), jnp.float32),
            pltpu.SemaphoreType.DMA((2,)),
            pltpu.SemaphoreType.DMA((2,)),
            pltpu.SemaphoreType.DMA((group,)),
            pltpu.SemaphoreType.DMA((group,)),
            pltpu.SemaphoreType.DMA((group,)),
            pltpu.SemaphoreType.DMA((group,)),
        ],
        compiler_params=pltpu.CompilerParams(
            collective_id=1, has_side_effects=True, vmem_limit_bytes=16 * 1024 * 1024
        ),
        name="sum_everywhere",
    )(grams)


def ritz_kernel(total_rows, gram_ref, y_ref, ky_ref, basis_ref, matrix_ref, image_ref, scaled, resid, factor):
    n = scaled.shape[0]
    row_id = lax.broadcasted_iota(jnp.int32, (n, n), 0)
    col_id = lax.broadcasted_iota(jnp.int32, (n, n), 1)
    unit = (row_id == col_id).astype(jnp.float32)
    gram = gram_ref[:n] * (1.0 / total_rows)
    on_diag = gram * unit
    down = 1.0 / jnp.sqrt(jnp.sum(on_diag, axis=1, keepdims=True))
    across = 1.0 / jnp.sqrt(jnp.sum(on_diag, axis=0, keepdims=True))
    scaled[...] = gram * down * across
    factor[...] = unit
    resid[...] = scaled[...] - unit

    def distance():
        return jnp.sum(resid[...] * resid[...])

    def improve():
        lower = jnp.where(row_id > col_id, resid[...], 0.0) + 0.5 * unit * resid[...]
        factor[...] = factor[...] - split3_dot(lower, factor[...], ((1,), (0,)))

    def step(state):
        improve()
        left = split3_dot(factor[...], scaled[...], ((1,), (0,)))
        resid[...] = split3_dot(left, factor[...], ((1,), (1,))) - unit
        return state[0] + 1, distance()

    _, left_over = lax.while_loop(
        lambda state: jnp.logical_and(state[0] < 8, state[1] > 1e-4), step, (jnp.int32(0), distance())
    )
    near = left_over <= 1e-4

    @pl.when(near)
    def _():
        improve()

    @pl.when(jnp.logical_not(near))
    def _():
        factor[...] = unit
        resid[...] = scaled[...]

        def eliminate(j, carry):
            row = resid[pl.ds(j, 1), :]
            lane = lax.broadcasted_iota(jnp.int32, (1, n), 1)
            pivot = jnp.sum(jnp.where(lane == j, row, 0.0), axis=1, keepdims=True)
            column = jnp.sum(jnp.where(col_id == j, resid[...], 0.0), axis=1, keepdims=True)
            place = lax.broadcasted_iota(jnp.int32, (n, 1), 0)
            ratio = jnp.where(place > j, column / pivot, 0.0)
            resid[...] = resid[...] - ratio * row
            mine = factor[pl.ds(j, 1), :]
            factor[...] = factor[...] - ratio * mine
            factor[pl.ds(j, 1), :] = mine / jnp.sqrt(pivot)
            return carry

        lax.fori_loop(0, n, eliminate, 0)

    inverse = factor[...] * across
    rows = y_ref.shape[0] * y_ref.shape[1]
    basis_ref[...] = split3_dot(y_ref[...].reshape(rows, n), inverse, ((1,), (1,))).reshape(basis_ref.shape)
    image_ref[...] = split3_dot(ky_ref[...].reshape(rows, n), inverse, ((1,), (1,))).reshape(image_ref.shape)
    left = split3_dot(inverse, gram_ref[n:] * (1.0 / total_rows), ((1,), (0,)))
    matrix_ref[...] = split3_dot(left, inverse, ((1,), (1,)))


def shards(slabs, rows, panel, blocks, offsets, stiff_diag, base_mass, mistune, pattern):
    _, cols, block_rows, vectors = panel.shape
    slots = blocks.shape[2]
    total_rows = cols * block_rows * slabs * rows
    levels = mistune.shape[0]
    one_hot = (pattern[:, :, None] == jnp.arange(levels, dtype=jnp.int32)).astype(jnp.float32)
    blade_factor = jnp.einsum("ijp,pb->ijb", one_hot, mistune, precision=highest)
    mass = (base_mass * blade_factor)[0]
    halves = 2
    lanes = vectors // halves
    spread = lambda a: jnp.broadcast_to(a[..., None], (cols, block_rows, lanes))
    vmem = pl.BlockSpec(memory_space=pltpu.VMEM)
    field = jax.ShapeDtypeStruct((cols, block_rows, vectors), jnp.float32)
    cells = 3 * (cols + 2)
    y, ky, grams = pl.pallas_call(
        functools.partial(filter_kernel, slabs, rows, cols, slots, halves, lanes),
        out_shape=(field, field, jax.ShapeDtypeStruct((2 * vectors, vectors), jnp.float32)),
        in_specs=[pl.BlockSpec(memory_space=pltpu.SMEM)] + [vmem] * 5,
        out_specs=(vmem, vmem, vmem),
        scratch_shapes=[pltpu.VMEM((cells, block_rows, lanes), jnp.bfloat16)] * 4
        + [
            pltpu.VMEM((cols, block_rows, vectors), jnp.float32),
            pltpu.SemaphoreType.DMA((2, halves, 2)),
            pltpu.SemaphoreType.DMA((2, halves, 2)),
            pltpu.SemaphoreType.DMA((2, halves, 2, 3)),
            pltpu.SemaphoreType.DMA((2, halves, 2, 3)),
        ],
        compiler_params=pltpu.CompilerParams(
            collective_id=0, has_side_effects=True, vmem_limit_bytes=32 * 1024 * 1024
        ),
        name="filter_and_grams",
    )(neighbour_index(offsets, cols), panel[0], blocks[0], spread(1.0 / mass), spread(stiff_diag[0]), spread(mass))
    grams = sum_everywhere(grams, slabs, rows)
    square = jax.ShapeDtypeStruct((vectors, vectors), jnp.float32)
    ritz_basis, ritz_matrix, stiff_image = pl.pallas_call(
        functools.partial(ritz_kernel, total_rows),
        out_shape=(field, square, field),
        in_specs=[vmem] * 3,
        out_specs=(vmem,) * 3,
        scratch_shapes=[pltpu.VMEM((vectors, vectors), jnp.float32)] * 3,
        compiler_params=pltpu.CompilerParams(vmem_limit_bytes=32 * 1024 * 1024),
        name="ritz",
    )(grams, y, ky)
    ritz_basis, stiff_image = ritz_basis[None], stiff_image[None]
    return (ritz_basis, ritz_matrix, stiff_image)


def solution(mesh):
    return jax.shard_map(
        functools.partial(shards, mesh.shape["slab"], mesh.shape["row"]),
        mesh=mesh,
        in_specs=(
            P("slab", "row", None, None),
            P("slab", "row", None, None, None),
            P("slab", "row", None),
            P("slab", "row", None),
            P("slab", "row", None),
            P(),
            P("slab", "row"),
        ),
        out_specs=(P("slab", "row", None, None), P(), P("slab", "row", None, None)),
        check_vma=False,
    )
```

```python
import functools

import jax
import jax.numpy as jnp
from jax import lax
from jax.experimental import pallas as pl
from jax.experimental.pallas import tpu as pltpu
from jax.sharding import PartitionSpec as P

DEG = 8
MESH = pl.DeviceIdType.MESH

highest = lax.Precision.HIGHEST
lower_edge = 2.5
upper_edge = 12.0
anchor_point = 0.0


def filter_scales(degree):
    half_width = (upper_edge - lower_edge) / 2.0
    centre_point = (upper_edge + lower_edge) / 2.0
    first_scale = half_width / (anchor_point - centre_point)
    doubled = 2.0 / first_scale
    scales = [(first_scale / half_width, 0.0)]
    previous = first_scale
    for section in range(1, degree):
        current = 1.0 / (doubled - previous)
        scales.append((2.0 * current / half_width, previous * current))
        previous = current
    return (centre_point, scales)


def neighbour_index(offsets, cross_blocks):
    cross_pos = jnp.arange(cross_blocks, dtype=jnp.int32)[None, :, None]
    return ((offsets // 3) * (cross_blocks + 2) + cross_pos + offsets % 3).reshape(-1)


def split3_dot(a, b, dims):
    a_hi = a.astype(jnp.bfloat16)
    b_hi = b.astype(jnp.bfloat16)
    a_lo = (a - a_hi.astype(jnp.float32)).astype(jnp.bfloat16)
    b_lo = (b - b_hi.astype(jnp.float32)).astype(jnp.bfloat16)
    dot = functools.partial(
        lax.dot_general, dimension_numbers=(dims, ((), ())), preferred_element_type=jnp.float32
    )
    return dot(a_hi, b_hi) + (dot(a_hi, b_lo) + dot(a_lo, b_hi))


def filter_kernel(
    slabs, rows, cols, slots, halves, lanes, fused,
    index_ref, panel_ref, blocks_ref, inv_ref, diag_ref, mass_ref,
    y_ref, ky_ref, gram_ref,
    ext00, ext01, ext10, ext11, prev_ref, slab_send, slab_recv, row_send, row_recv,
    *sum_refs,
):
    wide = cols + 2
    first = wide + 1
    ext = ((ext00, ext01), (ext10, ext11))
    s = lax.axis_index("slab")
    r = lax.axis_index("row")
    up = lax.rem(s + 1, slabs)
    down = lax.rem(s + slabs - 1, slabs)
    has_left = r > 0
    has_right = r < rows - 1
    centre, scales = filter_scales(DEG)

    vectors = y_ref.shape[-1]
    core = lax.rem(r, 2)
    group = slabs * (rows // 2)
    me = s * (rows // 2) + r // 2
    partner = (s, r + 1 - 2 * core)

    def member(d):
        q = lax.rem(me + d, group)
        return (q // (rows // 2), lax.rem(q, rows // 2) * 2 + core)

    barrier = pltpu.get_barrier_semaphore()
    if fused:
        greet_left = jnp.logical_and(has_left, core == 0)
        greet_right = jnp.logical_and(has_right, core == 1)
        pl.semaphore_signal(barrier, inc=1, device_id=partner, device_id_type=MESH)
        for d in range(1, group):
            pl.semaphore_signal(barrier, inc=1, device_id=member(d), device_id_type=MESH)
        others = group + (1 - core) * ((r + rows - 1) // rows) + core * ((2 * rows - 2 - r) // rows)
    else:
        greet_left, greet_right = has_left, has_right
        pl.semaphore_signal(barrier, inc=1, device_id=(up, r), device_id_type=MESH)
        pl.semaphore_signal(barrier, inc=1, device_id=(down, r), device_id_type=MESH)
        others = 2 + (r + rows - 1) // rows + (2 * rows - 2 - r) // rows

    @pl.when(greet_left)
    def _():
        pl.semaphore_signal(barrier, inc=1, device_id=(s, r - 1), device_id_type=MESH)

    @pl.when(greet_right)
    def _():
        pl.semaphore_signal(barrier, inc=1, device_id=(s, r + 1), device_id_type=MESH)

    if fused:
        local, folded, parts, total_sum, pair_send, pair_recv, a_send, a_recv, b_send, b_recv = sum_refs
        half = vectors // 2
        chunk = half // group
        mine = pl.ds(pl.multiple_of(core * half, half), half)
        theirs = pl.ds(pl.multiple_of((1 - core) * half, half), half)
        spot = pl.ds(pl.multiple_of(core * half + me * chunk, chunk), chunk)

        def swap_copy(m):
            return pltpu.make_async_remote_copy(
                src_ref=local.at[m, theirs], dst_ref=folded.at[m],
                send_sem=pair_send.at[m, 0], recv_sem=pair_recv.at[m, 0],
                device_id=partner, device_id_type=MESH,
            )

        def join_copy(m):
            return pltpu.make_async_remote_copy(
                src_ref=total_sum.at[m, mine], dst_ref=total_sum.at[m, mine],
                send_sem=pair_send.at[m, 1], recv_sem=pair_recv.at[m, 1],
                device_id=partner, device_id_type=MESH,
            )

        def scatter_copy(m, d):
            q = lax.rem(me + d, group)
            return pltpu.make_async_remote_copy(
                src_ref=folded.at[m, pl.ds(pl.multiple_of(q * chunk, chunk), chunk)], dst_ref=parts.at[m, d],
                send_sem=a_send.at[m, d], recv_sem=a_recv.at[m, d], device_id=member(d), device_id_type=MESH,
            )

        def spread_copy(m, d):
            return pltpu.make_async_remote_copy(
                src_ref=total_sum.at[m, spot], dst_ref=total_sum.at[m, spot],
                send_sem=b_send.at[m, d], recv_sem=b_recv.at[m, d], device_id=member(d), device_id_type=MESH,
            )

        def sum_begin(m, gram):
            local[m] = gram
            swap_copy(m).start()

        def sum_scatter(m):
            swap_copy(m).wait()
            folded[m] += local[m, mine]
            for d in range(1, group):
                scatter_copy(m, d).start()

        def sum_spread(m):
            acc = folded[m, pl.ds(pl.multiple_of(me * chunk, chunk), chunk)]
            for d in range(1, group):
                scatter_copy(m, d).wait()
                acc += parts[m, d]
            total_sum[m, spot] = acc
            for d in range(1, group):
                spread_copy(m, d).start()

        def sum_join(m):
            for d in range(1, group):
                spread_copy(m, d).wait()
            join_copy(m).start()

        def sum_end(m):
            join_copy(m).wait()
            gram_ref[m * vectors:(m + 1) * vectors] = total_sum[m]

    def slab_copies(t):
        p, h = (t // halves) % 2, t % halves
        buf = ext[p][h]
        own = buf.at[pl.ds(first, cols)]
        return [
            pltpu.make_async_remote_copy(
                src_ref=own, dst_ref=buf.at[pl.ds(1 + 2 * wide * lower, cols)],
                send_sem=slab_send.at[p, h, lower], recv_sem=slab_recv.at[p, h, lower],
                device_id=(target, r), device_id_type=MESH,
            )
            for lower, target in ((0, up), (1, down))
        ]

    def row_copies(t, side):
        p, h = (t // halves) % 2, t % halves
        buf = ext[p][h]
        source, place, target = ((cols, 0, r + 1), (1, cols + 1, r - 1))[side]
        return [
            pltpu.make_async_remote_copy(
                src_ref=buf.at[pl.ds(source + wide * k, 1)], dst_ref=buf.at[pl.ds(place + wide * k, 1)],
                send_sem=row_send.at[p, h, side, k], recv_sem=row_recv.at[p, h, side, k],
                device_id=(s, target), device_id_type=MESH,
            )
            for k in range(3)
        ]

    def start_slab(t):
        for copy in slab_copies(t):
            copy.start()

    def wait_slab(t):
        for copy in slab_copies(t):
            copy.wait()

    def start_row(t):
        for side, there in ((0, has_right), (1, has_left)):
            @pl.when(there)
            def _():
                for copy in row_copies(t, side):
                    copy.start()

    def wait_row(t):
        for side, there in ((0, has_right), (1, has_left)):
            @pl.when(there)
            def _():
                for copy in row_copies(t, side):
                    copy.wait_send()
                for copy in row_copies(t, 1 - side):
                    copy.wait_recv()

    def compute(t):
        k, h = t // halves, t % halves
        buf = ext[k % 2][h]
        nxt = ext[(k + 1) % 2][h]
        span = pl.ds(h * lanes, lanes)

        def one(c, carry):
            acc = diag_ref[c] * buf[first + c].astype(jnp.float32) if k < DEG else diag_ref[c] * y_ref[c, :, span]
            for slot in range(slots):
                acc += jnp.dot(
                    blocks_ref[c, slot], buf[index_ref[c * slots + slot]], preferred_element_type=jnp.float32
                )
            if k < DEG:
                gain, back = scales[k]
                cur = y_ref[c, :, span]
                new = gain * (inv_ref[c] * acc - centre * cur)
                if k > 0:
                    new -= back * prev_ref[c, :, span]
                prev_ref[c, :, span] = cur
                y_ref[c, :, span] = new
                nxt[first + c] = new.astype(jnp.bfloat16)
            else:
                ky_ref[c, :, span] = acc
            return carry

        lax.fori_loop(0, cols, one, 0)

    for p in range(2):
        for h in range(halves):
            @pl.when(jnp.logical_not(has_left))
            def _():
                for k in range(3):
                    ext[p][h][wide * k] = jnp.zeros(ext00.shape[1:], jnp.bfloat16)

            @pl.when(jnp.logical_not(has_right))
            def _():
                for k in range(3):
                    ext[p][h][wide * k + cols + 1] = jnp.zeros(ext00.shape[1:], jnp.bfloat16)

    for h in range(halves):
        for c in range(cols):
            ext[0][h][first + c] = panel_ref[c, :, h * lanes:(h + 1) * lanes]

    pl.semaphore_wait(barrier, others)

    for h in range(halves):
        start_slab(h)
    y_ref[...] = panel_ref[...].astype(jnp.float32)
    total = halves * (DEG + 1)
    depth = cols * y_ref.shape[1]
    last = halves * DEG
    for t in range(total + 1):
        if fused and t == last + 2:
            sum_spread(0)
        if t >= 1:
            wait_row(t - 1)
            compute(t - 1)
            if halves <= t - 1 + halves < total:
                start_slab(t - 1 + halves)
            if t == last:
                flat = y_ref[...].reshape(depth, vectors)
                weight = mass_ref[...].reshape(depth, lanes)
                weighted = jnp.concatenate([weight] * halves, axis=1) * flat
                gram = split3_dot(weighted, flat, ((0,), (0,)))
                if fused:
                    sum_begin(0, gram)
                else:
                    gram_ref[:vectors] = gram
            if fused and t == last + 1:
                sum_scatter(0)
        if t < total:
            wait_slab(t)
            start_row(t)
    gram = split3_dot(
        y_ref[...].reshape(depth, vectors), ky_ref[...].reshape(depth, vectors), ((0,), (0,))
    )
    if fused:
        sum_begin(1, gram)
        sum_join(0)
        sum_scatter(1)
        sum_end(0)
        sum_spread(1)
        sum_join(1)
        sum_end(1)
    else:
        gram_ref[vectors:] = gram


def ritz_kernel(total_rows, gram_ref, y_ref, ky_ref, basis_ref, matrix_ref, image_ref, scaled, resid, factor):
    n = scaled.shape[0]
    row_id = lax.broadcasted_iota(jnp.int32, (n, n), 0)
    col_id = lax.broadcasted_iota(jnp.int32, (n, n), 1)
    unit = (row_id == col_id).astype(jnp.float32)
    gram = gram_ref[:n] * (1.0 / total_rows)
    on_diag = gram * unit
    down = 1.0 / jnp.sqrt(jnp.sum(on_diag, axis=1, keepdims=True))
    across = 1.0 / jnp.sqrt(jnp.sum(on_diag, axis=0, keepdims=True))
    scaled[...] = gram * down * across
    factor[...] = unit
    resid[...] = scaled[...] - unit

    def distance():
        return jnp.sum(resid[...] * resid[...])

    def improve():
        lower = jnp.where(row_id > col_id, resid[...], 0.0) + 0.5 * unit * resid[...]
        factor[...] = factor[...] - split3_dot(lower, factor[...], ((1,), (0,)))

    def step(state):
        improve()
        left = split3_dot(factor[...], scaled[...], ((1,), (0,)))
        resid[...] = split3_dot(left, factor[...], ((1,), (1,))) - unit
        return state[0] + 1, distance()

    _, left_over = lax.while_loop(
        lambda state: jnp.logical_and(state[0] < 8, state[1] > 1e-4), step, (jnp.int32(0), distance())
    )
    near = left_over <= 1e-4

    @pl.when(near)
    def _():
        improve()

    @pl.when(jnp.logical_not(near))
    def _():
        factor[...] = unit
        resid[...] = scaled[...]

        def eliminate(j, carry):
            row = resid[pl.ds(j, 1), :]
            lane = lax.broadcasted_iota(jnp.int32, (1, n), 1)
            pivot = jnp.sum(jnp.where(lane == j, row, 0.0), axis=1, keepdims=True)
            column = jnp.sum(jnp.where(col_id == j, resid[...], 0.0), axis=1, keepdims=True)
            place = lax.broadcasted_iota(jnp.int32, (n, 1), 0)
            ratio = jnp.where(place > j, column / pivot, 0.0)
            resid[...] = resid[...] - ratio * row
            mine = factor[pl.ds(j, 1), :]
            factor[...] = factor[...] - ratio * mine
            factor[pl.ds(j, 1), :] = mine / jnp.sqrt(pivot)
            return carry

        lax.fori_loop(0, n, eliminate, 0)

    inverse = factor[...] * across
    rows = y_ref.shape[0] * y_ref.shape[1]
    basis_ref[...] = split3_dot(y_ref[...].reshape(rows, n), inverse, ((1,), (1,))).reshape(basis_ref.shape)
    image_ref[...] = split3_dot(ky_ref[...].reshape(rows, n), inverse, ((1,), (1,))).reshape(image_ref.shape)
    left = split3_dot(inverse, gram_ref[n:] * (1.0 / total_rows), ((1,), (0,)))
    matrix_ref[...] = split3_dot(left, inverse, ((1,), (1,)))


def shards(slabs, rows, panel, blocks, offsets, stiff_diag, base_mass, mistune, pattern):
    _, cols, block_rows, vectors = panel.shape
    slots = blocks.shape[2]
    total_rows = cols * block_rows * slabs * rows
    levels = mistune.shape[0]
    one_hot = (pattern[:, :, None] == jnp.arange(levels, dtype=jnp.int32)).astype(jnp.float32)
    blade_factor = jnp.einsum("ijp,pb->ijb", one_hot, mistune, precision=highest)
    mass = (base_mass * blade_factor)[0]
    halves = 2
    lanes = vectors // halves
    spread = lambda a: jnp.broadcast_to(a[..., None], (cols, block_rows, lanes))
    vmem = pl.BlockSpec(memory_space=pltpu.VMEM)
    field = jax.ShapeDtypeStruct((cols, block_rows, vectors), jnp.float32)
    cells = 3 * (cols + 2)
    group = slabs * (rows // 2)
    half = vectors // 2
    fused = halves == 2 and rows % 2 == 0 and half % group == 0 and (half // group) % 8 == 0
    sum_scratch = [
        pltpu.VMEM((2, vectors, vectors), jnp.float32),
        pltpu.VMEM((2, half, vectors), jnp.float32),
        pltpu.VMEM((2, group, half // group, vectors), jnp.float32),
        pltpu.VMEM((2, vectors, vectors), jnp.float32),
        pltpu.SemaphoreType.DMA((2, 2)),
        pltpu.SemaphoreType.DMA((2, 2)),
    ] + [pltpu.SemaphoreType.DMA((2, group))] * 4
    y, ky, grams = pl.pallas_call(
        functools.partial(filter_kernel, slabs, rows, cols, slots, halves, lanes, fused),
        out_shape=(field, field, jax.ShapeDtypeStruct((2 * vectors, vectors), jnp.float32)),
        in_specs=[pl.BlockSpec(memory_space=pltpu.SMEM)] + [vmem] * 5,
        out_specs=(vmem, vmem, vmem),
        scratch_shapes=[pltpu.VMEM((cells, block_rows, lanes), jnp.bfloat16)] * 4
        + [
            pltpu.VMEM((cols, block_rows, vectors), jnp.float32),
            pltpu.SemaphoreType.DMA((2, halves, 2)),
            pltpu.SemaphoreType.DMA((2, halves, 2)),
            pltpu.SemaphoreType.DMA((2, halves, 2, 3)),
            pltpu.SemaphoreType.DMA((2, halves, 2, 3)),
        ]
        + (sum_scratch if fused else []),
        compiler_params=pltpu.CompilerParams(
            collective_id=0, has_side_effects=True, vmem_limit_bytes=32 * 1024 * 1024
        ),
        name="filter_and_grams",
    )(neighbour_index(offsets, cols), panel[0], blocks[0], spread(1.0 / mass), spread(stiff_diag[0]), spread(mass))
    if not fused:
        grams = lax.psum(grams, ("slab", "row"))
    square = jax.ShapeDtypeStruct((vectors, vectors), jnp.float32)
    ritz_basis, ritz_matrix, stiff_image = pl.pallas_call(
        functools.partial(ritz_kernel, total_rows),
        out_shape=(field, square, field),
        in_specs=[vmem] * 3,
        out_specs=(vmem,) * 3,
        scratch_shapes=[pltpu.VMEM((vectors, vectors), jnp.float32)] * 3,
        compiler_params=pltpu.CompilerParams(vmem_limit_bytes=32 * 1024 * 1024),
        name="ritz",
    )(grams, y, ky)
    ritz_basis, stiff_image = ritz_basis[None], stiff_image[None]
    return (ritz_basis, ritz_matrix, stiff_image)


def solution(mesh):
    return jax.shard_map(
        functools.partial(shards, mesh.shape["slab"], mesh.shape["row"]),
        mesh=mesh,
        in_specs=(
            P("slab", "row", None, None),
            P("slab", "row", None, None, None),
            P("slab", "row", None),
            P("slab", "row", None),
            P("slab", "row", None),
            P(),
            P("slab", "row"),
        ),
        out_specs=(P("slab", "row", None, None), P(), P("slab", "row", None, None)),
        check_vma=False,
    )
```

```python
import functools

import jax
import jax.numpy as jnp
from jax import lax
from jax.experimental import pallas as pl
from jax.experimental.pallas import tpu as pltpu
from jax.sharding import PartitionSpec as P

DEG = 8
MESH = pl.DeviceIdType.MESH

highest = lax.Precision.HIGHEST
lower_edge = 2.5
upper_edge = 12.0
anchor_point = 0.0


def filter_scales(degree):
    half_width = (upper_edge - lower_edge) / 2.0
    centre_point = (upper_edge + lower_edge) / 2.0
    first_scale = half_width / (anchor_point - centre_point)
    doubled = 2.0 / first_scale
    scales = [(first_scale / half_width, 0.0)]
    previous = first_scale
    for section in range(1, degree):
        current = 1.0 / (doubled - previous)
        scales.append((2.0 * current / half_width, previous * current))
        previous = current
    return (centre_point, scales)


def neighbour_index(offsets, cross_blocks):
    cross_pos = jnp.arange(cross_blocks, dtype=jnp.int32)[None, :, None]
    return ((offsets // 3) * (cross_blocks + 2) + cross_pos + offsets % 3).reshape(-1)


def split3_dot(a, b, dims):
    a_hi = a.astype(jnp.bfloat16)
    b_hi = b.astype(jnp.bfloat16)
    a_lo = (a - a_hi.astype(jnp.float32)).astype(jnp.bfloat16)
    b_lo = (b - b_hi.astype(jnp.float32)).astype(jnp.bfloat16)
    dot = functools.partial(
        lax.dot_general, dimension_numbers=(dims, ((), ())), preferred_element_type=jnp.float32
    )
    return dot(a_hi, b_hi) + (dot(a_hi, b_lo) + dot(a_lo, b_hi))


def filter_kernel(
    slabs, rows, cols, slots, halves, lanes, fused,
    index_ref, panel_ref, blocks_ref, inv_ref, diag_ref, mass_ref,
    y_ref, ky_ref, gram_ref,
    ext00, ext01, ext10, ext11, prev_ref, slab_send, slab_recv, row_send, row_recv,
    *sum_refs,
):
    wide = cols + 2
    first = wide + 1
    ext = ((ext00, ext01), (ext10, ext11))
    s = lax.axis_index("slab")
    r = lax.axis_index("row")
    up = lax.rem(s + 1, slabs)
    down = lax.rem(s + slabs - 1, slabs)
    has_left = r > 0
    has_right = r < rows - 1
    centre, scales = filter_scales(DEG)

    vectors = y_ref.shape[-1]
    core = lax.rem(r, 2)
    group = slabs * (rows // 2)
    me = s * (rows // 2) + r // 2
    partner = (s, r + 1 - 2 * core)

    def member(d):
        q = lax.rem(me + d, group)
        return (q // (rows // 2), lax.rem(q, rows // 2) * 2 + core)

    barrier = pltpu.get_barrier_semaphore()
    if fused:
        greet_left = jnp.logical_and(has_left, core == 0)
        greet_right = jnp.logical_and(has_right, core == 1)
        pl.semaphore_signal(barrier, inc=1, device_id=partner, device_id_type=MESH)
        for d in range(1, group):
            pl.semaphore_signal(barrier, inc=1, device_id=member(d), device_id_type=MESH)
        others = group + (1 - core) * ((r + rows - 1) // rows) + core * ((2 * rows - 2 - r) // rows)
    else:
        greet_left, greet_right = has_left, has_right
        pl.semaphore_signal(barrier, inc=1, device_id=(up, r), device_id_type=MESH)
        pl.semaphore_signal(barrier, inc=1, device_id=(down, r), device_id_type=MESH)
        others = 2 + (r + rows - 1) // rows + (2 * rows - 2 - r) // rows

    @pl.when(greet_left)
    def _():
        pl.semaphore_signal(barrier, inc=1, device_id=(s, r - 1), device_id_type=MESH)

    @pl.when(greet_right)
    def _():
        pl.semaphore_signal(barrier, inc=1, device_id=(s, r + 1), device_id_type=MESH)

    if fused:
        local, folded, parts, total_sum, pair_send, pair_recv, a_send, a_recv, b_send, b_recv = sum_refs
        half = vectors // 2
        chunk = half // group
        mine = pl.ds(pl.multiple_of(core * half, half), half)
        theirs = pl.ds(pl.multiple_of((1 - core) * half, half), half)
        spot = pl.ds(pl.multiple_of(core * half + me * chunk, chunk), chunk)

        def swap_copy(m):
            return pltpu.make_async_remote_copy(
                src_ref=local.at[m, theirs], dst_ref=folded.at[m],
                send_sem=pair_send.at[m, 0], recv_sem=pair_recv.at[m, 0],
                device_id=partner, device_id_type=MESH,
            )

        def join_copy(m):
            return pltpu.make_async_remote_copy(
                src_ref=total_sum.at[m, mine], dst_ref=total_sum.at[m, mine],
                send_sem=pair_send.at[m, 1], recv_sem=pair_recv.at[m, 1],
                device_id=partner, device_id_type=MESH,
            )

        def scatter_copy(m, d):
            q = lax.rem(me + d, group)
            return pltpu.make_async_remote_copy(
                src_ref=folded.at[m, pl.ds(pl.multiple_of(q * chunk, chunk), chunk)], dst_ref=parts.at[m, d],
                send_sem=a_send.at[m, d], recv_sem=a_recv.at[m, d], device_id=member(d), device_id_type=MESH,
            )

        def spread_copy(m, d):
            return pltpu.make_async_remote_copy(
                src_ref=total_sum.at[m, spot], dst_ref=total_sum.at[m, spot],
                send_sem=b_send.at[m, d], recv_sem=b_recv.at[m, d], device_id=member(d), device_id_type=MESH,
            )

        def sum_begin(m, gram):
            local[m] = gram
            swap_copy(m).start()

        def sum_scatter(m):
            swap_copy(m).wait()
            folded[m] += local[m, mine]
            for d in range(1, group):
                scatter_copy(m, d).start()

        def sum_spread(m):
            acc = folded[m, pl.ds(pl.multiple_of(me * chunk, chunk), chunk)]
            for d in range(1, group):
                scatter_copy(m, d).wait()
                acc += parts[m, d]
            total_sum[m, spot] = acc
            for d in range(1, group):
                spread_copy(m, d).start()

        def sum_join(m):
            for d in range(1, group):
                spread_copy(m, d).wait()
            join_copy(m).start()

        def sum_end(m):
            join_copy(m).wait()
            gram_ref[m * vectors:(m + 1) * vectors] = total_sum[m]

    def slab_copies(t):
        p, h = (t // halves) % 2, t % halves
        buf = ext[p][h]
        own = buf.at[pl.ds(first, cols)]
        return [
            pltpu.make_async_remote_copy(
                src_ref=own, dst_ref=buf.at[pl.ds(1 + 2 * wide * lower, cols)],
                send_sem=slab_send.at[p, h, lower], recv_sem=slab_recv.at[p, h, lower],
                device_id=(target, r), device_id_type=MESH,
            )
            for lower, target in ((0, up), (1, down))
        ]

    def row_copies(t, side):
        p, h = (t // halves) % 2, t % halves
        buf = ext[p][h]
        source, place, target = ((cols, 0, r + 1), (1, cols + 1, r - 1))[side]
        return [
            pltpu.make_async_remote_copy(
                src_ref=buf.at[pl.ds(source + wide * k, 1)], dst_ref=buf.at[pl.ds(place + wide * k, 1)],
                send_sem=row_send.at[p, h, side, k], recv_sem=row_recv.at[p, h, side, k],
                device_id=(s, target), device_id_type=MESH,
            )
            for k in range(3)
        ]

    def start_slab(t):
        for copy in slab_copies(t):
            copy.start()
        start_row(t, (1,))

    def wait_slab(t):
        for copy in slab_copies(t):
            copy.wait()

    def start_row(t, which):
        for side, there in ((0, has_right), (1, has_left)):
            @pl.when(there)
            def _():
                copies = row_copies(t, side)
                for k in which:
                    copies[k].start()

    def wait_row(t):
        for side, there in ((0, has_right), (1, has_left)):
            @pl.when(there)
            def _():
                for copy in row_copies(t, side):
                    copy.wait_send()
                for copy in row_copies(t, 1 - side):
                    copy.wait_recv()

    def compute(t):
        k, h = t // halves, t % halves
        buf = ext[k % 2][h]
        nxt = ext[(k + 1) % 2][h]
        span = pl.ds(h * lanes, lanes)

        def one(c, carry):
            acc = diag_ref[c] * buf[first + c].astype(jnp.float32) if k < DEG else diag_ref[c] * y_ref[c, :, span]
            for slot in range(slots):
                acc += jnp.dot(
                    blocks_ref[c, slot], buf[index_ref[c * slots + slot]], preferred_element_type=jnp.float32
                )
            if k < DEG:
                gain, back = scales[k]
                cur = y_ref[c, :, span]
                new = gain * (inv_ref[c] * acc - centre * cur)
                if k > 0:
                    new -= back * prev_ref[c, :, span]
                prev_ref[c, :, span] = cur
                y_ref[c, :, span] = new
                nxt[first + c] = new.astype(jnp.bfloat16)
            else:
                ky_ref[c, :, span] = acc
            return carry

        lax.fori_loop(0, cols, one, 0)

    for p in range(2):
        for h in range(halves):
            @pl.when(jnp.logical_not(has_left))
            def _():
                for k in range(3):
                    ext[p][h][wide * k] = jnp.zeros(ext00.shape[1:], jnp.bfloat16)

            @pl.when(jnp.logical_not(has_right))
            def _():
                for k in range(3):
                    ext[p][h][wide * k + cols + 1] = jnp.zeros(ext00.shape[1:], jnp.bfloat16)

    for h in range(halves):
        for c in range(cols):
            ext[0][h][first + c] = panel_ref[c, :, h * lanes:(h + 1) * lanes]

    pl.semaphore_wait(barrier, others)

    for h in range(halves):
        start_slab(h)
    y_ref[...] = panel_ref[...].astype(jnp.float32)
    total = halves * (DEG + 1)
    depth = cols * y_ref.shape[1]
    last = halves * DEG
    for t in range(total + 1):
        if t >= 1:
            wait_row(t - 1)
            compute(t - 1)
            if halves <= t - 1 + halves < total:
                start_slab(t - 1 + halves)
            if t == last:
                flat = y_ref[...].reshape(depth, vectors)
                weight = mass_ref[...].reshape(depth, lanes)
                weighted = jnp.concatenate([weight] * halves, axis=1) * flat
                gram = split3_dot(weighted, flat, ((0,), (0,)))
                if fused:
                    sum_begin(0, gram)
                else:
                    gram_ref[:vectors] = gram
            if fused and t == last + 1:
                sum_scatter(0)
        if t < total:
            wait_slab(t)
            start_row(t, (0, 2))
    gram = split3_dot(
        y_ref[...].reshape(depth, vectors), ky_ref[...].reshape(depth, vectors), ((0,), (0,))
    )
    if fused:
        sum_begin(1, gram)
        sum_spread(0)
        sum_scatter(1)
        sum_join(0)
        sum_spread(1)
        sum_join(1)
        sum_end(0)
        sum_end(1)
    else:
        gram_ref[vectors:] = gram


def ritz_kernel(total_rows, gram_ref, y_ref, ky_ref, basis_ref, matrix_ref, image_ref, scaled, resid, factor):
    n = scaled.shape[0]
    row_id = lax.broadcasted_iota(jnp.int32, (n, n), 0)
    col_id = lax.broadcasted_iota(jnp.int32, (n, n), 1)
    unit = (row_id == col_id).astype(jnp.float32)
    gram = gram_ref[:n] * (1.0 / total_rows)
    on_diag = gram * unit
    down = 1.0 / jnp.sqrt(jnp.sum(on_diag, axis=1, keepdims=True))
    across = 1.0 / jnp.sqrt(jnp.sum(on_diag, axis=0, keepdims=True))
    scaled[...] = gram * down * across
    factor[...] = unit
    resid[...] = scaled[...] - unit

    def distance():
        return jnp.sum(resid[...] * resid[...])

    def improve():
        lower = jnp.where(row_id > col_id, resid[...], 0.0) + 0.5 * unit * resid[...]
        factor[...] = factor[...] - split3_dot(lower, factor[...], ((1,), (0,)))

    def step(state):
        improve()
        left = split3_dot(factor[...], scaled[...], ((1,), (0,)))
        resid[...] = split3_dot(left, factor[...], ((1,), (1,))) - unit
        return state[0] + 1, distance()

    _, left_over = lax.while_loop(
        lambda state: jnp.logical_and(state[0] < 8, state[1] > 1e-4), step, (jnp.int32(0), distance())
    )
    near = left_over <= 1e-4

    @pl.when(near)
    def _():
        improve()

    @pl.when(jnp.logical_not(near))
    def _():
        factor[...] = unit
        resid[...] = scaled[...]

        def eliminate(j, carry):
            row = resid[pl.ds(j, 1), :]
            lane = lax.broadcasted_iota(jnp.int32, (1, n), 1)
            pivot = jnp.sum(jnp.where(lane == j, row, 0.0), axis=1, keepdims=True)
            column = jnp.sum(jnp.where(col_id == j, resid[...], 0.0), axis=1, keepdims=True)
            place = lax.broadcasted_iota(jnp.int32, (n, 1), 0)
            ratio = jnp.where(place > j, column / pivot, 0.0)
            resid[...] = resid[...] - ratio * row
            mine = factor[pl.ds(j, 1), :]
            factor[...] = factor[...] - ratio * mine
            factor[pl.ds(j, 1), :] = mine / jnp.sqrt(pivot)
            return carry

        lax.fori_loop(0, n, eliminate, 0)

    inverse = factor[...] * across
    rows = y_ref.shape[0] * y_ref.shape[1]
    basis_ref[...] = split3_dot(y_ref[...].reshape(rows, n), inverse, ((1,), (1,))).reshape(basis_ref.shape)
    image_ref[...] = split3_dot(ky_ref[...].reshape(rows, n), inverse, ((1,), (1,))).reshape(image_ref.shape)
    left = split3_dot(inverse, gram_ref[n:] * (1.0 / total_rows), ((1,), (0,)))
    matrix_ref[...] = split3_dot(left, inverse, ((1,), (1,)))


def shards(slabs, rows, panel, blocks, offsets, stiff_diag, base_mass, mistune, pattern):
    _, cols, block_rows, vectors = panel.shape
    slots = blocks.shape[2]
    total_rows = cols * block_rows * slabs * rows
    levels = mistune.shape[0]
    one_hot = (pattern[:, :, None] == jnp.arange(levels, dtype=jnp.int32)).astype(jnp.float32)
    blade_factor = jnp.einsum("ijp,pb->ijb", one_hot, mistune, precision=highest)
    mass = (base_mass * blade_factor)[0]
    halves = 2
    lanes = vectors // halves
    spread = lambda a: jnp.broadcast_to(a[..., None], (cols, block_rows, lanes))
    vmem = pl.BlockSpec(memory_space=pltpu.VMEM)
    field = jax.ShapeDtypeStruct((cols, block_rows, vectors), jnp.float32)
    cells = 3 * (cols + 2)
    group = slabs * (rows // 2)
    half = vectors // 2
    fused = halves == 2 and rows % 2 == 0 and half % group == 0 and (half // group) % 8 == 0
    sum_scratch = [
        pltpu.VMEM((2, vectors, vectors), jnp.float32),
        pltpu.VMEM((2, half, vectors), jnp.float32),
        pltpu.VMEM((2, group, half // group, vectors), jnp.float32),
        pltpu.VMEM((2, vectors, vectors), jnp.float32),
        pltpu.SemaphoreType.DMA((2, 2)),
        pltpu.SemaphoreType.DMA((2, 2)),
    ] + [pltpu.SemaphoreType.DMA((2, group))] * 4
    y, ky, grams = pl.pallas_call(
        functools.partial(filter_kernel, slabs, rows, cols, slots, halves, lanes, fused),
        out_shape=(field, field, jax.ShapeDtypeStruct((2 * vectors, vectors), jnp.float32)),
        in_specs=[pl.BlockSpec(memory_space=pltpu.SMEM)] + [vmem] * 5,
        out_specs=(vmem, vmem, vmem),
        scratch_shapes=[pltpu.VMEM((cells, block_rows, lanes), jnp.bfloat16)] * 4
        + [
            pltpu.VMEM((cols, block_rows, vectors), jnp.float32),
            pltpu.SemaphoreType.DMA((2, halves, 2)),
            pltpu.SemaphoreType.DMA((2, halves, 2)),
            pltpu.SemaphoreType.DMA((2, halves, 2, 3)),
            pltpu.SemaphoreType.DMA((2, halves, 2, 3)),
        ]
        + (sum_scratch if fused else []),
        compiler_params=pltpu.CompilerParams(
            collective_id=0, has_side_effects=True, vmem_limit_bytes=32 * 1024 * 1024
        ),
        name="filter_and_grams",
    )(neighbour_index(offsets, cols), panel[0], blocks[0], spread(1.0 / mass), spread(stiff_diag[0]), spread(mass))
    if not fused:
        grams = lax.psum(grams, ("slab", "row"))
    square = jax.ShapeDtypeStruct((vectors, vectors), jnp.float32)
    ritz_basis, ritz_matrix, stiff_image = pl.pallas_call(
        functools.partial(ritz_kernel, total_rows),
        out_shape=(field, square, field),
        in_specs=[vmem] * 3,
        out_specs=(vmem,) * 3,
        scratch_shapes=[pltpu.VMEM((vectors, vectors), jnp.float32)] * 3,
        compiler_params=pltpu.CompilerParams(vmem_limit_bytes=32 * 1024 * 1024),
        name="ritz",
    )(grams, y, ky)
    ritz_basis, stiff_image = ritz_basis[None], stiff_image[None]
    return (ritz_basis, ritz_matrix, stiff_image)


def solution(mesh):
    return jax.shard_map(
        functools.partial(shards, mesh.shape["slab"], mesh.shape["row"]),
        mesh=mesh,
        in_specs=(
            P("slab", "row", None, None),
            P("slab", "row", None, None, None),
            P("slab", "row", None),
            P("slab", "row", None),
            P("slab", "row", None),
            P(),
            P("slab", "row"),
        ),
        out_specs=(P("slab", "row", None, None), P(), P("slab", "row", None, None)),
        check_vma=False,
    )
```

```python
import functools

import jax
import jax.numpy as jnp
from jax import lax
from jax.experimental import pallas as pl
from jax.experimental.pallas import tpu as pltpu
from jax.sharding import PartitionSpec as P

DEG = 8
MESH = pl.DeviceIdType.MESH

highest = lax.Precision.HIGHEST
lower_edge = 2.5
upper_edge = 12.0
anchor_point = 0.0


def filter_scales(degree):
    half_width = (upper_edge - lower_edge) / 2.0
    centre_point = (upper_edge + lower_edge) / 2.0
    first_scale = half_width / (anchor_point - centre_point)
    doubled = 2.0 / first_scale
    scales = [(first_scale / half_width, 0.0)]
    previous = first_scale
    for section in range(1, degree):
        current = 1.0 / (doubled - previous)
        scales.append((2.0 * current / half_width, previous * current))
        previous = current
    return (centre_point, scales)


def neighbour_index(offsets, cross_blocks):
    cross_pos = jnp.arange(cross_blocks, dtype=jnp.int32)[None, :, None]
    return ((offsets // 3) * (cross_blocks + 2) + cross_pos + offsets % 3).reshape(-1)


def split3_dot(a, b, dims):
    a_hi = a.astype(jnp.bfloat16)
    b_hi = b.astype(jnp.bfloat16)
    a_lo = (a - a_hi.astype(jnp.float32)).astype(jnp.bfloat16)
    b_lo = (b - b_hi.astype(jnp.float32)).astype(jnp.bfloat16)
    dot = functools.partial(
        lax.dot_general, dimension_numbers=(dims, ((), ())), preferred_element_type=jnp.float32
    )
    return dot(a_hi, b_hi) + (dot(a_hi, b_lo) + dot(a_lo, b_hi))


def filter_kernel(
    slabs, rows, cols, slots, halves, lanes, fused,
    index_ref, panel_ref, blocks_ref, inv_ref, diag_ref, mass_ref,
    y_ref, ky_ref, gram_ref,
    ext00, ext01, ext10, ext11, prev_ref, slab_send, slab_recv, row_send, row_recv,
    *sum_refs,
):
    wide = cols + 2
    first = wide + 1
    ext = ((ext00, ext01), (ext10, ext11))
    s = lax.axis_index("slab")
    r = lax.axis_index("row")
    up = lax.rem(s + 1, slabs)
    down = lax.rem(s + slabs - 1, slabs)
    has_left = r > 0
    has_right = r < rows - 1
    centre, scales = filter_scales(DEG)

    vectors = y_ref.shape[-1]
    core = lax.rem(r, 2)
    group = slabs * (rows // 2)
    me = s * (rows // 2) + r // 2
    partner = (s, r + 1 - 2 * core)

    def member(d):
        q = lax.rem(me + d, group)
        return (q // (rows // 2), lax.rem(q, rows // 2) * 2 + core)

    barrier = pltpu.get_barrier_semaphore()
    if fused:
        greet_left = jnp.logical_and(has_left, core == 0)
        greet_right = jnp.logical_and(has_right, core == 1)
        pl.semaphore_signal(barrier, inc=1, device_id=partner, device_id_type=MESH)
        for d in range(1, group):
            pl.semaphore_signal(barrier, inc=1, device_id=member(d), device_id_type=MESH)
        others = group + (1 - core) * ((r + rows - 1) // rows) + core * ((2 * rows - 2 - r) // rows)
    else:
        greet_left, greet_right = has_left, has_right
        pl.semaphore_signal(barrier, inc=1, device_id=(up, r), device_id_type=MESH)
        pl.semaphore_signal(barrier, inc=1, device_id=(down, r), device_id_type=MESH)
        others = 2 + (r + rows - 1) // rows + (2 * rows - 2 - r) // rows

    @pl.when(greet_left)
    def _():
        pl.semaphore_signal(barrier, inc=1, device_id=(s, r - 1), device_id_type=MESH)

    @pl.when(greet_right)
    def _():
        pl.semaphore_signal(barrier, inc=1, device_id=(s, r + 1), device_id_type=MESH)

    if fused:
        local, folded, parts, total_sum, pair_send, pair_recv, a_send, a_recv, b_send, b_recv = sum_refs
        half = vectors // 2
        chunk = half // group
        mine = pl.ds(pl.multiple_of(core * half, half), half)
        theirs = pl.ds(pl.multiple_of((1 - core) * half, half), half)
        spot = pl.ds(pl.multiple_of(core * half + me * chunk, chunk), chunk)

        def swap_copy(m):
            return pltpu.make_async_remote_copy(
                src_ref=local.at[m, theirs], dst_ref=folded.at[m],
                send_sem=pair_send.at[m, 0], recv_sem=pair_recv.at[m, 0],
                device_id=partner, device_id_type=MESH,
            )

        def join_copy(m):
            return pltpu.make_async_remote_copy(
                src_ref=total_sum.at[m, mine], dst_ref=total_sum.at[m, mine],
                send_sem=pair_send.at[m, 1], recv_sem=pair_recv.at[m, 1],
                device_id=partner, device_id_type=MESH,
            )

        def scatter_copy(m, d):
            q = lax.rem(me + d, group)
            return pltpu.make_async_remote_copy(
                src_ref=folded.at[m, pl.ds(pl.multiple_of(q * chunk, chunk), chunk)], dst_ref=parts.at[m, d],
                send_sem=a_send.at[m, d], recv_sem=a_recv.at[m, d], device_id=member(d), device_id_type=MESH,
            )

        def spread_copy(m, d):
            return pltpu.make_async_remote_copy(
                src_ref=total_sum.at[m, spot], dst_ref=total_sum.at[m, spot],
                send_sem=b_send.at[m, d], recv_sem=b_recv.at[m, d], device_id=member(d), device_id_type=MESH,
            )

        def sum_begin(m, gram):
            local[m] = gram
            swap_copy(m).start()

        def sum_scatter(m):
            swap_copy(m).wait()
            folded[m] += local[m, mine]
            for d in range(1, group):
                scatter_copy(m, d).start()

        def sum_spread(m):
            acc = folded[m, pl.ds(pl.multiple_of(me * chunk, chunk), chunk)]
            for d in range(1, group):
                scatter_copy(m, d).wait()
                acc += parts[m, d]
            total_sum[m, spot] = acc
            for d in range(1, group):
                spread_copy(m, d).start()

        def sum_join(m):
            for d in range(1, group):
                spread_copy(m, d).wait()
            join_copy(m).start()

        def sum_end(m):
            join_copy(m).wait()
            gram_ref[m * vectors:(m + 1) * vectors] = total_sum[m]

    def slab_copies(t):
        p, h = (t // halves) % 2, t % halves
        buf = ext[p][h]
        own = buf.at[pl.ds(first, cols)]
        return [
            pltpu.make_async_remote_copy(
                src_ref=own, dst_ref=buf.at[pl.ds(1 + 2 * wide * lower, cols)],
                send_sem=slab_send.at[p, h, lower], recv_sem=slab_recv.at[p, h, lower],
                device_id=(target, r), device_id_type=MESH,
            )
            for lower, target in ((0, up), (1, down))
        ]

    def row_copies(t, side):
        p, h = (t // halves) % 2, t % halves
        buf = ext[p][h]
        source, place, target = ((cols, 0, lax.rem(r + 1, rows)), (1, cols + 1, lax.rem(r + rows - 1, rows)))[side]
        return [
            pltpu.make_async_remote_copy(
                src_ref=buf.at[pl.ds(source + wide * k, 1)], dst_ref=buf.at[pl.ds(place + wide * k, 1)],
                send_sem=row_send.at[p, h, side, k], recv_sem=row_recv.at[p, h, side, k],
                device_id=(s, target), device_id_type=MESH,
            )
            for k in range(3)
        ]

    def start_slab(t):
        for copy in slab_copies(t):
            copy.start()
        start_row(t, (1,))

    def wait_slab(t):
        for copy in slab_copies(t):
            copy.wait()

    def start_row(t, which):
        for side, there in ((0, has_right), (1, has_left)):
            @pl.when(there)
            def _():
                copies = row_copies(t, side)
                for k in which:
                    copies[k].start()

    def wait_row(t):
        for side, there in ((0, has_right), (1, has_left)):
            @pl.when(there)
            def _():
                for copy in row_copies(t, side):
                    copy.wait_send()
                for copy in row_copies(t, 1 - side):
                    copy.wait_recv()

    def compute(t):
        k, h = t // halves, t % halves
        buf = ext[k % 2][h]
        nxt = ext[(k + 1) % 2][h]
        span = pl.ds(h * lanes, lanes)

        def one(c, carry):
            acc = diag_ref[c] * buf[first + c].astype(jnp.float32) if k < DEG else diag_ref[c] * y_ref[c, :, span]
            for slot in range(slots):
                acc += jnp.dot(
                    blocks_ref[c, slot], buf[index_ref[c * slots + slot]], preferred_element_type=jnp.float32
                )
            if k < DEG:
                gain, back = scales[k]
                cur = y_ref[c, :, span]
                new = gain * (inv_ref[c] * acc - centre * cur)
                if k > 0:
                    new -= back * prev_ref[c, :, span]
                prev_ref[c, :, span] = cur
                y_ref[c, :, span] = new
                nxt[first + c] = new.astype(jnp.bfloat16)
            else:
                ky_ref[c, :, span] = acc
            return carry

        lax.fori_loop(0, cols, one, 0)

    for p in range(2):
        for h in range(halves):
            @pl.when(jnp.logical_not(has_left))
            def _():
                for k in range(3):
                    ext[p][h][wide * k] = jnp.zeros(ext00.shape[1:], jnp.bfloat16)

            @pl.when(jnp.logical_not(has_right))
            def _():
                for k in range(3):
                    ext[p][h][wide * k + cols + 1] = jnp.zeros(ext00.shape[1:], jnp.bfloat16)

    for h in range(halves):
        for c in range(cols):
            ext[0][h][first + c] = panel_ref[c, :, h * lanes:(h + 1) * lanes]

    pl.semaphore_wait(barrier, others)

    for h in range(halves):
        start_slab(h)
    y_ref[...] = panel_ref[...].astype(jnp.float32)
    total = halves * (DEG + 1)
    depth = cols * y_ref.shape[1]
    last = halves * DEG
    for t in range(total + 1):
        if t >= 1:
            wait_row(t - 1)
            compute(t - 1)
            if halves <= t - 1 + halves < total:
                start_slab(t - 1 + halves)
            if t == last:
                flat = y_ref[...].reshape(depth, vectors)
                weight = mass_ref[...].reshape(depth, lanes)
                weighted = jnp.concatenate([weight] * halves, axis=1) * flat
                gram = split3_dot(weighted, flat, ((0,), (0,)))
                if fused:
                    sum_begin(0, gram)
                else:
                    gram_ref[:vectors] = gram
            if fused and t == last + 1:
                sum_scatter(0)
        if t < total:
            wait_slab(t)
            start_row(t, (0, 2))
    gram = split3_dot(
        y_ref[...].reshape(depth, vectors), ky_ref[...].reshape(depth, vectors), ((0,), (0,))
    )
    if fused:
        sum_begin(1, gram)
        sum_spread(0)
        sum_scatter(1)
        sum_join(0)
        sum_spread(1)
        sum_join(1)
        sum_end(0)
        sum_end(1)
    else:
        gram_ref[vectors:] = gram


def ritz_kernel(total_rows, gram_ref, y_ref, ky_ref, basis_ref, matrix_ref, image_ref, scaled, resid, factor):
    n = scaled.shape[0]
    row_id = lax.broadcasted_iota(jnp.int32, (n, n), 0)
    col_id = lax.broadcasted_iota(jnp.int32, (n, n), 1)
    unit = (row_id == col_id).astype(jnp.float32)
    gram = gram_ref[:n] * (1.0 / total_rows)
    on_diag = gram * unit
    down = 1.0 / jnp.sqrt(jnp.sum(on_diag, axis=1, keepdims=True))
    across = 1.0 / jnp.sqrt(jnp.sum(on_diag, axis=0, keepdims=True))
    scaled[...] = gram * down * across
    factor[...] = unit
    resid[...] = scaled[...] - unit

    def distance():
        return jnp.sum(resid[...] * resid[...])

    def improve():
        lower = jnp.where(row_id > col_id, resid[...], 0.0) + 0.5 * unit * resid[...]
        factor[...] = factor[...] - split3_dot(lower, factor[...], ((1,), (0,)))

    def step(state):
        improve()
        left = split3_dot(factor[...], scaled[...], ((1,), (0,)))
        resid[...] = split3_dot(left, factor[...], ((1,), (1,))) - unit
        return state[0] + 1, distance()

    _, left_over = lax.while_loop(
        lambda state: jnp.logical_and(state[0] < 8, state[1] > 1e-4), step, (jnp.int32(0), distance())
    )
    near = left_over <= 1e-4

    @pl.when(near)
    def _():
        improve()

    @pl.when(jnp.logical_not(near))
    def _():
        factor[...] = unit
        resid[...] = scaled[...]

        def eliminate(j, carry):
            row = resid[pl.ds(j, 1), :]
            lane = lax.broadcasted_iota(jnp.int32, (1, n), 1)
            pivot = jnp.sum(jnp.where(lane == j, row, 0.0), axis=1, keepdims=True)
            column = jnp.sum(jnp.where(col_id == j, resid[...], 0.0), axis=1, keepdims=True)
            place = lax.broadcasted_iota(jnp.int32, (n, 1), 0)
            ratio = jnp.where(place > j, column / pivot, 0.0)
            resid[...] = resid[...] - ratio * row
            mine = factor[pl.ds(j, 1), :]
            factor[...] = factor[...] - ratio * mine
            factor[pl.ds(j, 1), :] = mine / jnp.sqrt(pivot)
            return carry

        lax.fori_loop(0, n, eliminate, 0)

    inverse = factor[...] * across
    rows = y_ref.shape[0] * y_ref.shape[1]
    basis_ref[...] = split3_dot(y_ref[...].reshape(rows, n), inverse, ((1,), (1,))).reshape(basis_ref.shape)
    image_ref[...] = split3_dot(ky_ref[...].reshape(rows, n), inverse, ((1,), (1,))).reshape(image_ref.shape)
    left = split3_dot(inverse, gram_ref[n:] * (1.0 / total_rows), ((1,), (0,)))
    matrix_ref[...] = split3_dot(left, inverse, ((1,), (1,)))


def shards(slabs, rows, panel, blocks, offsets, stiff_diag, base_mass, mistune, pattern):
    _, cols, block_rows, vectors = panel.shape
    slots = blocks.shape[2]
    total_rows = cols * block_rows * slabs * rows
    levels = mistune.shape[0]
    one_hot = (pattern[:, :, None] == jnp.arange(levels, dtype=jnp.int32)).astype(jnp.float32)
    blade_factor = jnp.einsum("ijp,pb->ijb", one_hot, mistune, precision=highest)
    mass = (base_mass * blade_factor)[0]
    halves = 2
    lanes = vectors // halves
    spread = lambda a: jnp.broadcast_to(a[..., None], (cols, block_rows, lanes))
    vmem = pl.BlockSpec(memory_space=pltpu.VMEM)
    field = jax.ShapeDtypeStruct((cols, block_rows, vectors), jnp.float32)
    cells = 3 * (cols + 2)
    group = slabs * (rows // 2)
    half = vectors // 2
    fused = halves == 2 and rows % 2 == 0 and half % group == 0 and (half // group) % 8 == 0
    sum_scratch = [
        pltpu.VMEM((2, vectors, vectors), jnp.float32),
        pltpu.VMEM((2, half, vectors), jnp.float32),
        pltpu.VMEM((2, group, half // group, vectors), jnp.float32),
        pltpu.VMEM((2, vectors, vectors), jnp.float32),
        pltpu.SemaphoreType.DMA((2, 2)),
        pltpu.SemaphoreType.DMA((2, 2)),
    ] + [pltpu.SemaphoreType.DMA((2, group))] * 4
    y, ky, grams = pl.pallas_call(
        functools.partial(filter_kernel, slabs, rows, cols, slots, halves, lanes, fused),
        out_shape=(field, field, jax.ShapeDtypeStruct((2 * vectors, vectors), jnp.float32)),
        in_specs=[pl.BlockSpec(memory_space=pltpu.SMEM)] + [vmem] * 5,
        out_specs=(vmem, vmem, vmem),
        scratch_shapes=[pltpu.VMEM((cells, block_rows, lanes), jnp.bfloat16)] * 4
        + [
            pltpu.VMEM((cols, block_rows, vectors), jnp.float32),
            pltpu.SemaphoreType.DMA((2, halves, 2)),
            pltpu.SemaphoreType.DMA((2, halves, 2)),
            pltpu.SemaphoreType.DMA((2, halves, 2, 3)),
            pltpu.SemaphoreType.DMA((2, halves, 2, 3)),
        ]
        + (sum_scratch if fused else []),
        compiler_params=pltpu.CompilerParams(
            collective_id=0, has_side_effects=True, vmem_limit_bytes=32 * 1024 * 1024
        ),
        name="filter_and_grams",
    )(neighbour_index(offsets, cols), panel[0], blocks[0], spread(1.0 / mass), spread(stiff_diag[0]), spread(mass))
    if not fused:
        grams = lax.psum(grams, ("slab", "row"))
    square = jax.ShapeDtypeStruct((vectors, vectors), jnp.float32)
    ritz_basis, ritz_matrix, stiff_image = pl.pallas_call(
        functools.partial(ritz_kernel, total_rows),
        out_shape=(field, square, field),
        in_specs=[vmem] * 3,
        out_specs=(vmem,) * 3,
        scratch_shapes=[pltpu.VMEM((vectors, vectors), jnp.float32)] * 3,
        compiler_params=pltpu.CompilerParams(vmem_limit_bytes=32 * 1024 * 1024),
        name="ritz",
    )(grams, y, ky)
    ritz_basis, stiff_image = ritz_basis[None], stiff_image[None]
    return (ritz_basis, ritz_matrix, stiff_image)


def solution(mesh):
    return jax.shard_map(
        functools.partial(shards, mesh.shape["slab"], mesh.shape["row"]),
        mesh=mesh,
        in_specs=(
            P("slab", "row", None, None),
            P("slab", "row", None, None, None),
            P("slab", "row", None),
            P("slab", "row", None),
            P("slab", "row", None),
            P(),
            P("slab", "row"),
        ),
        out_specs=(P("slab", "row", None, None), P(), P("slab", "row", None, None)),
        check_vma=False,
    )
```
